256 devices in a mesh: pool: 32 (over y, x, core), tp: 8 (over z).
Axes of the slice: x: 4, y: 4, z: 8, core: 2. Of those that a mesh axis runs over, the one named last changes fastest.
Arguments:
- turn_query: bfloat16 [16384, 4096], P('pool', 'tp'), may hold values from -16 to 16
- turn_key: bfloat16 [16384, 1024], P('pool', 'tp'), may hold values from -16 to 16, as said below
- turn_value: bfloat16 [16384, 1024], P('pool', 'tp'), may hold values from -6 to 6
- pool_keys: bfloat16 [2048, 128, 1024], P('pool', None, 'tp'), may hold values from -16 to 16, as said below
- pool_values: bfloat16 [2048, 128, 1024], P('pool', None, 'tp'), may hold values from -6 to 6
- seat_session: int32 [64], replicated, may hold values from 0 to 63, as said below
- history_len: int32 [64], replicated, may hold values from 1 to 4096, as said below
- block_map: int32 [64, 32], replicated, may hold values from 0 to 2047, as said below
- out_weight: bfloat16 [4096, 8192], P('tp', 'pool'), may hold values from -0.1875 to 0.1875
Outputs:
- layer_out: bfloat16 [16384, 8192], P('pool', 'tp')
The draws below stay inside these ranges and needn't reach their ends.
Inputs may be any that keep to these rules, and one draw needn't show every extreme that they name: `seat_session`: A permutation of the sessions. `history_len`: the sessions of one owner, chosen afresh in every draw, have length 4096. Every slot of the pool is named exactly once. Call block j of session s live when j * 128 < history_len[s]; the slot's pool index is block_map[s, j] // 64. The live blocks of one pool index that belong to the sessions of one owner number at most 2; some owner receives exactly 2 from every pool index. `turn_key`: Real-valued keys. `pool_keys`: Real-valued keys; slots not named by a live block hold values that are never read.
All inputs are finite; a program needn't handle non-finite values.
Results may differ from the reference program's by a relative error of at most 0.019.
Values may be sent and summed in bfloat16 or wider, within the bound.
No kernel may reach another device: no remote copies, remote signals or barrier semaphores. Data moves between devices by JAX's collectives and lax.ppermute only.
A program may use at most 128 MiB of HBM per device.

```python
import math
import jax
import jax.numpy as jnp
from jax import lax

D = 8192
HD = 128
QH_DEV = 4
NEW = 256
SESS_DEV = 2
BT = 128
MAXBLK = 32
QHEADS = 32
KVHEADS = 8
SESSIONS = 64
ROWS = 16384
HISTMAX = 4096
BLK_DEV = 64
SLOTS = 2048
N_POOL = 32
N_TP = 8


def layout_ints(key):
    sub_keys = jax.random.split(key, 6)
    seating = jax.random.permutation(sub_keys[0], SESSIONS).astype(jnp.int32)
    first_len = jax.random.randint(sub_keys[1], (SESSIONS,), 0, HISTMAX, dtype=jnp.int32)
    second_len = jax.random.randint(sub_keys[2], (SESSIONS,), 0, HISTMAX, dtype=jnp.int32)
    lengths = jnp.minimum(first_len, second_len) + 1
    busiest = jax.random.randint(sub_keys[3], (), 0, N_POOL, dtype=jnp.int32)
    chosen = seating[busiest * SESS_DEV + jnp.arange(SESS_DEV, dtype=jnp.int32)]
    lengths = lengths.at[chosen].set(HISTMAX)
    orders = jax.vmap(lambda sub_key: jax.random.permutation(sub_key, MAXBLK))(jax.random.split(sub_keys[4], SESSIONS)).astype(jnp.int32)
    device_of = orders % N_POOL
    within = orders // N_POOL
    reserved = jnp.arange(SESSIONS, dtype=jnp.int32)[:, None] * (MAXBLK // N_POOL) + within
    shuffles = jax.vmap(lambda sub_key: jax.random.permutation(sub_key, BLK_DEV))(jax.random.split(sub_keys[5], N_POOL)).astype(jnp.int32)
    local_slot = shuffles[device_of, reserved]
    mapping = device_of * BLK_DEV + local_slot
    return (seating, lengths, mapping)


def draw_seat_session(key, part):
    seating, lengths, mapping = layout_ints(key)
    return seating


def draw_history_len(key, part):
    seating, lengths, mapping = layout_ints(key)
    return lengths


def draw_block_map(key, part):
    seating, lengths, mapping = layout_ints(key)
    return mapping


def draw_pool_keys(key, part):
    key = jax.random.fold_in(key, 11)
    sub_keys = jax.random.split(key, 2)
    shape = (SLOTS, BT, KVHEADS * HD)
    values = jax.random.truncated_normal(sub_keys[1], -6.0, 6.0, shape)
    return values.astype(jnp.bfloat16)


def draw_turn_key(key, part):
    key = jax.random.fold_in(key, 12)
    sub_keys = jax.random.split(key, 2)
    shape = (ROWS, KVHEADS * HD)
    values = jax.random.truncated_normal(sub_keys[1], -6.0, 6.0, shape)
    return values.astype(jnp.bfloat16)


def draw_turn_query(key, part):
    key = jax.random.fold_in(key, 13)
    sub_keys = jax.random.split(key, 2)
    shape = (ROWS, QHEADS * HD)
    values = jax.random.truncated_normal(sub_keys[1], -6.0, 6.0, shape)
    return values.astype(jnp.bfloat16)


def strengthened(drawn, stream_key, source, target, blocks, factor):
    owner, partner = [(jnp.arange(drawn.shape[dim]) // (drawn.shape[dim] // blocks)).reshape([-1 if axis == dim else 1 for axis in range(drawn.ndim)]) for dim in (source, target)]
    chosen = jax.random.permutation(stream_key, blocks)[partner]
    strong = (owner == chosen) | (owner == (partner + blocks // 2) % blocks)
    return jnp.where(strong, factor * drawn, drawn)


def levels(own_key, extent, cuts, low, top_value):
    loudness, own = 1.0, jax.random.fold_in(own_key, 6)
    for dim, blocks in cuts:
        steps = jnp.exp(jax.random.uniform(jax.random.fold_in(own, dim), (blocks,), jnp.float32, low / len(cuts), top_value / len(cuts)))
        loudness = loudness * jnp.repeat(steps, extent[dim] // blocks).reshape([-1 if axis == dim else 1 for axis in range(len(extent))])
    return loudness


def gaussian(own_key, dims, width, most, shards=(), kind=jnp.bfloat16):
    gain = levels(own_key, dims, shards, -0.22, 0.18) if shards else 1.0
    array = jax.random.normal(own_key, dims, jnp.float32) * width * gain
    return jnp.minimum(jnp.maximum(array, -most), most).astype(kind)


def heavy_noise(own_key, dims, width, most, shards, heavy, kind=jnp.bfloat16):
    drawn = width * jax.random.normal(own_key, dims, jnp.float32)
    if shards:
        drawn = drawn * levels(own_key, dims, shards, -0.22, 0.18)
    return jnp.clip(strengthened(drawn, jax.random.fold_in(own_key, 3), *heavy), -most, most).astype(kind)


def setup_inputs(seed: int = 0) -> dict:
    keys = jax.random.split(jax.random.key(seed), 10)
    turn_query = draw_turn_query(jax.random.fold_in(keys[9], 71), 0)
    turn_key = draw_turn_key(jax.random.fold_in(keys[9], 71), 0)
    turn_value = gaussian(keys[2], (ROWS, KVHEADS * HD), 1.0, 6.0, ((0, 32), (1, 8)))
    pool_keys = draw_pool_keys(jax.random.fold_in(keys[9], 71), 0)
    pool_values = gaussian(keys[4], (SLOTS, BT, KVHEADS * HD), 1.0, 6.0, ((0, 32), (2, 8)))
    seat_session = draw_seat_session(jax.random.fold_in(keys[9], 71), 0)
    history_len = draw_history_len(jax.random.fold_in(keys[9], 71), 0)
    block_map = draw_block_map(jax.random.fold_in(keys[9], 71), 0)
    out_weight = heavy_noise(keys[8], (QHEADS * HD, D), (QHEADS * HD) ** -0.5, 0.1875, ((0, 8), (1, 32)), (0, 1, 32, 2.75))
    return dict(turn_query=turn_query, turn_key=turn_key, turn_value=turn_value, pool_keys=pool_keys, pool_values=pool_values, seat_session=seat_session, history_len=history_len, block_map=block_map, out_weight=out_weight)


rope_base = 1000000.0

def rotate(values, positions):
    half_dim = values.shape[-1] // 2
    freq_index = jnp.arange(half_dim, dtype=jnp.float32)
    inverse = rope_base ** (-2.0 * freq_index / values.shape[-1])
    angles = positions.astype(jnp.float32)[:, None, None] * inverse[None, None, :]
    cosine = jnp.cos(angles)
    sine_part = jnp.sin(angles)
    lower_half = values[..., :half_dim]
    upper_half = values[..., half_dim:]
    return jnp.concatenate([lower_half * cosine - upper_half * sine_part, upper_half * cosine + lower_half * sine_part], axis=-1)

def narrow(values):
    return lax.optimization_barrier(values.astype(jnp.bfloat16))

def reference(turn_query, turn_key, turn_value, pool_keys, pool_values, seat_session, history_len, block_map, out_weight):
    scaling = 1.0 / math.sqrt(HD)

    def one_seat(seat_number):
        session = seat_session[seat_number]
        length = history_len[session]
        slot_ids = block_map[session]
        hist_keys = pool_keys[slot_ids].reshape(HISTMAX, KVHEADS, HD)
        hist_vals = pool_values[slot_ids].reshape(HISTMAX, KVHEADS, HD)
        row_start = (seat_number * NEW).astype(jnp.int32)
        queries = lax.dynamic_slice_in_dim(turn_query, row_start, NEW, 0).reshape(NEW, QHEADS, HD)
        new_keys = lax.dynamic_slice_in_dim(turn_key, row_start, NEW, 0).reshape(NEW, KVHEADS, HD)
        new_vals = lax.dynamic_slice_in_dim(turn_value, row_start, NEW, 0).reshape(NEW, KVHEADS, HD)
        turn_pos = length + jnp.arange(NEW, dtype=jnp.int32)
        hist_pos = jnp.arange(HISTMAX, dtype=jnp.int32)
        roped_query = narrow(rotate(queries.astype(jnp.float32), turn_pos))
        roped_keys = narrow(jnp.concatenate([rotate(hist_keys.astype(jnp.float32), hist_pos), rotate(new_keys.astype(jnp.float32), turn_pos)], axis=0))
        all_vals = jnp.concatenate([hist_vals, new_vals], axis=0)
        grouped = roped_query.reshape(NEW, KVHEADS, QH_DEV, HD)
        scores = jnp.einsum('tgqd,kgd->tgqk', grouped.astype(jnp.float32), roped_keys.astype(jnp.float32)) * scaling
        key_index = jnp.arange(HISTMAX + NEW, dtype=jnp.int32)[None, :]
        token_index = jnp.arange(NEW, dtype=jnp.int32)[:, None]
        visible = jnp.where(key_index < HISTMAX, key_index < length, key_index - HISTMAX <= token_index)
        scores = jnp.where(visible[:, None, None, :], scores, -jnp.inf)
        row_top = lax.optimization_barrier(jnp.max(scores, axis=-1, keepdims=True))
        weights = jnp.exp(scores - row_top)
        denominator = lax.optimization_barrier(jnp.sum(weights, axis=-1, keepdims=True))
        weighted = jnp.einsum('tgqk,kgd->tgqd', narrow(weights).astype(jnp.float32), all_vals.astype(jnp.float32))
        return (weighted / denominator).astype(jnp.bfloat16).reshape(NEW, QHEADS * HD)
    attended = lax.map(one_seat, jnp.arange(SESSIONS, dtype=jnp.int32)).reshape(ROWS, QHEADS * HD)
    running = jnp.zeros((ROWS, D), jnp.float32)
    width_group = QH_DEV * HD
    for group_number in range(N_TP):
        col_lo = group_number * width_group
        partial_value = jnp.dot(attended[:, col_lo:col_lo + width_group], out_weight[col_lo:col_lo + width_group], preferred_element_type=jnp.float32)
        running = running + narrow(partial_value).astype(jnp.float32)
    return running.astype(jnp.bfloat16)
```

```python
import functools
import math

import jax
import jax.numpy as jnp
from jax import lax
from jax.experimental import pallas as pl
from jax.experimental.pallas import tpu as pltpu
from jax.sharding import PartitionSpec as P

rope_base = 1000000.0
CHUNK_BLOCKS = 8


def inverse_frequencies(head_dim):
    half_dim = head_dim // 2
    freq_index = jnp.arange(half_dim, dtype=jnp.float32)
    return rope_base ** (-2.0 * freq_index / head_dim)


def angle_tables(positions, head_dim):
    angles = positions.astype(jnp.float32)[:, None] * inverse_frequencies(head_dim)[None, :]
    cosine, sine = jnp.cos(angles), jnp.sin(angles)
    return jnp.concatenate([cosine, cosine], axis=1), jnp.concatenate([-sine, sine], axis=1)


def rotate_halves(values):
    half_dim = values.shape[-1] // 2
    return jnp.concatenate([values[..., half_dim:], values[..., :half_dim]], axis=-1)


def send_kernel(slot_ref, keys_ref, vals_ref, out_ref, sem):
    count = out_ref.shape[0]

    @pl.loop(0, count)
    def _(i):
        slot = slot_ref[i]
        pltpu.make_async_copy(keys_ref.at[slot], out_ref.at[i, 0], sem.at[0]).start()
        pltpu.make_async_copy(vals_ref.at[slot], out_ref.at[i, 1], sem.at[0]).start()

    pltpu.make_async_copy(out_ref, out_ref, sem.at[0]).wait()


def gather_send(slot_table, pool_keys, pool_values):
    count = slot_table.shape[0]
    return pl.pallas_call(
        send_kernel,
        out_shape=jax.ShapeDtypeStruct((count, 2) + pool_keys.shape[1:], pool_keys.dtype),
        grid_spec=pltpu.PrefetchScalarGridSpec(
            num_scalar_prefetch=1,
            grid=(1,),
            in_specs=[pl.BlockSpec(memory_space=pl.ANY)] * 2,
            out_specs=pl.BlockSpec(memory_space=pl.ANY),
            scratch_shapes=[pltpu.SemaphoreType.DMA((1,))],
        ),
    )(slot_table, pool_keys, pool_values)


def attention_kernel(
    seat,
    index_ref,
    length_ref,
    query_ref,
    turn_key_ref,
    turn_val_ref,
    row_cos_ref,
    row_sin_ref,
    base_cos_ref,
    base_sin_ref,
    arrived_ref,
    out_ref,
    blocks,
    roped,
    top_ref,
    total_ref,
    acc_ref,
    sems,
):
    heads, turn_len, head_dim = query_ref.shape
    block_count, _, block_rows, _ = blocks.shape
    chunk_rows = CHUNK_BLOCKS * block_rows
    scaling = math.log2(math.e) / math.sqrt(head_dim)
    length = length_ref[seat]
    chunks = pl.cdiv(length, chunk_rows)
    full = length // chunk_rows

    def copy(j):
        return pltpu.make_async_copy(
            arrived_ref.at[index_ref[seat * block_count + j]], blocks.at[j], sems.at[j]
        )

    @pl.loop(0, chunks * CHUNK_BLOCKS)
    def _(j):
        copy(j).start()

    def scores(h, keys):
        return lax.dot_general(
            query_ref[h], keys, (((1,), (1,)), ((), ())), preferred_element_type=jnp.float32
        )

    rows = lax.broadcasted_iota(jnp.int32, (turn_len, turn_len), 0)
    cols = lax.broadcasted_iota(jnp.int32, (turn_len, turn_len), 1)
    for h in range(heads):
        s = jnp.where(cols <= rows, scores(h, turn_key_ref[...]), -jnp.inf)
        top = jnp.max(s, axis=1, keepdims=True)
        weight = jnp.exp2((s - top) * scaling)
        top_ref[h] = top
        total_ref[h] = jnp.sum(weight, axis=1, keepdims=True)
        acc_ref[h] = jnp.dot(
            weight.astype(jnp.bfloat16), turn_val_ref[...], preferred_element_type=jnp.float32
        )

    def chunk_step(c, masked):
        for i in range(CHUNK_BLOCKS):
            j = c * CHUNK_BLOCKS + i
            copy(j).wait()
            base_cos = base_cos_ref[pl.ds(j, 1), :]
            base_sin = base_sin_ref[pl.ds(j, 1), :]
            row_cos, row_sin = row_cos_ref[...], row_sin_ref[...]
            cosine = row_cos * base_cos - row_sin * base_sin
            sine = row_sin * base_cos + row_cos * base_sin
            key = blocks[j, 0].astype(jnp.float32)
            key = key * cosine + pltpu.roll(key, head_dim // 2, 1) * sine
            roped[i * block_rows : (i + 1) * block_rows, :] = key.astype(jnp.bfloat16)
        vals = blocks[pl.ds(c * CHUNK_BLOCKS, CHUNK_BLOCKS), 1].reshape(chunk_rows, head_dim)
        keys = roped[...]
        for h in range(heads):
            s = scores(h, keys)
            if masked:
                place = c * chunk_rows + lax.broadcasted_iota(jnp.int32, s.shape, 1)
                s = jnp.where(place < length, s, -jnp.inf)
            old = top_ref[h]
            top = jnp.maximum(old, jnp.max(s, axis=1, keepdims=True))
            weight = jnp.exp2((s - top) * scaling)
            fade = jnp.exp2((old - top) * scaling)
            top_ref[h] = top
            total_ref[h] = total_ref[h] * fade + jnp.sum(weight, axis=1, keepdims=True)
            acc_ref[h] = acc_ref[h] * fade + jnp.dot(
                weight.astype(jnp.bfloat16), vals, preferred_element_type=jnp.float32
            )

    @pl.loop(0, full)
    def _(c):
        chunk_step(c, False)

    @pl.when(full < chunks)
    def _():
        chunk_step(full, True)

    for h in range(heads):
        out_ref[:, h * head_dim : (h + 1) * head_dim] = (acc_ref[h] / total_ref[h]).astype(
            jnp.bfloat16
        )


def attend(seat, recv_index, lengths, query, turn_key, turn_val, tables, arrived):
    heads, turn_len, head_dim = query.shape
    block_rows = arrived.shape[2]
    block_count = recv_index.shape[0] // lengths.shape[0]
    vmem = pl.BlockSpec(memory_space=pltpu.VMEM)
    return pl.pallas_call(
        functools.partial(attention_kernel, seat),
        out_shape=jax.ShapeDtypeStruct((turn_len, heads * head_dim), jnp.bfloat16),
        grid_spec=pltpu.PrefetchScalarGridSpec(
            num_scalar_prefetch=2,
            grid=(1,),
            in_specs=[vmem] * 7 + [pl.BlockSpec(memory_space=pl.ANY)],
            out_specs=vmem,
            scratch_shapes=[
                pltpu.VMEM((block_count, 2, block_rows, head_dim), jnp.bfloat16),
                pltpu.VMEM((CHUNK_BLOCKS * block_rows, head_dim), jnp.bfloat16),
                pltpu.VMEM((heads, turn_len, 1), jnp.float32),
                pltpu.VMEM((heads, turn_len, 1), jnp.float32),
                pltpu.VMEM((heads, turn_len, head_dim), jnp.float32),
                pltpu.SemaphoreType.DMA((block_count,)),
            ],
        ),
        compiler_params=pltpu.CompilerParams(vmem_limit_bytes=40 * 1024 * 1024),
        cost_estimate=pl.CostEstimate(
            flops=4 * heads * turn_len * (block_count * block_rows + turn_len) * head_dim,
            bytes_accessed=2 * 1024 * 1024,
            transcendentals=heads * turn_len * (block_count * block_rows + turn_len),
        ),
    )(recv_index, lengths, query, turn_key, turn_val, *tables, arrived)


def project_kernel(order_ref, rows_ref, weight_ref, out_ref, acc_ref):
    step = pl.program_id(0)
    pieces, _, width = weight_ref.shape
    for j in range(pieces):
        part = jnp.dot(rows_ref[0], weight_ref[j], preferred_element_type=jnp.float32)
        cols = slice(j * width, (j + 1) * width)

        @pl.when(step == 0)
        def _():
            acc_ref[:, cols] = part

        @pl.when(step > 0)
        def _():
            acc_ref[:, cols] += part

    @pl.when(step == pl.num_programs(0) - 1)
    def _():
        out_ref[...] = acc_ref[...].astype(jnp.bfloat16)


def project(order, gathered, weights):
    groups, rows, depth = gathered.shape
    pieces = weights.shape[0] // groups
    width = weights.shape[2]
    return pl.pallas_call(
        project_kernel,
        out_shape=jax.ShapeDtypeStruct((rows, pieces * width), jnp.bfloat16),
        grid_spec=pltpu.PrefetchScalarGridSpec(
            num_scalar_prefetch=1,
            grid=(groups,),
            in_specs=[
                pl.BlockSpec((1, rows, depth), lambda u, order: (order[u], 0, 0)),
                pl.BlockSpec((pieces, depth, width), lambda u, order: (u, 0, 0)),
            ],
            out_specs=pl.BlockSpec((rows, pieces * width), lambda u, order: (0, 0)),
            scratch_shapes=[pltpu.VMEM((rows, pieces * width), jnp.float32)],
        ),
        compiler_params=pltpu.CompilerParams(vmem_limit_bytes=40 * 1024 * 1024),
    )(order, gathered, weights)


def local(
    turn_query,
    turn_key,
    turn_value,
    pool_keys,
    pool_values,
    seat_session,
    history_len,
    block_map,
    out_weight,
):
    pooled_count = lax.axis_size("pool")
    tp_count = lax.axis_size("tp")
    current_index = lax.axis_index("pool")
    tp_index = lax.axis_index("tp")
    blocks_here, rows_per_block, head_dim = pool_keys.shape
    block_count = block_map.shape[1]
    per_owner = seat_session.shape[0] // pooled_count
    capacity = per_owner * block_count // pooled_count
    element_count = per_owner * block_count
    turn_len = turn_query.shape[0] // per_owner
    group_size = turn_query.shape[1] // head_dim
    pieces = pooled_count // tp_count

    seat_length = history_len[seat_session]
    seat_map = block_map[seat_session]
    seats_per_device = (seat_map // blocks_here).reshape(pooled_count, element_count)
    seat_slot = (seat_map % blocks_here).reshape(pooled_count, element_count)
    block_numbers = jnp.arange(block_count, dtype=jnp.int32)
    alive_flags = (block_numbers[None, :] * rows_per_block < seat_length[:, None]).reshape(
        pooled_count, element_count
    )
    departing_rows = alive_flags & (seats_per_device == current_index)
    send_rank = jnp.cumsum(departing_rows.astype(jnp.int32), axis=1) - 1
    selected = departing_rows[:, None, :] & (
        send_rank[:, None, :] == jnp.arange(capacity, dtype=jnp.int32)[None, :, None]
    )
    slot_table = jnp.sum(jnp.where(selected, seat_slot[:, None, :], 0), axis=2).reshape(
        pooled_count * capacity
    )
    sent = gather_send(slot_table, pool_keys, pool_values)
    arrived = lax.all_to_all(sent, "pool", split_axis=0, concat_axis=0, tiled=True)

    moves = []
    for p in range(pooled_count):
        for t in range(tp_count):
            plane = p // pieces
            place = (plane ^ t) * pieces + p % pieces
            moves.append((p * tp_count + t, place * tp_count + plane))
    moved = lax.ppermute(out_weight, ("pool", "tp"), moves)
    weights = lax.all_gather(moved, "pool", axis=0, tiled=False)

    own_lengths = lax.dynamic_slice_in_dim(seat_length, current_index * per_owner, per_owner, 0)
    home_dev = lax.dynamic_slice_in_dim(seats_per_device, current_index, 1, 0)[0]
    resident_alive = lax.dynamic_slice_in_dim(alive_flags, current_index, 1, 0)[0]
    sources = jnp.arange(pooled_count, dtype=jnp.int32)[:, None]
    arriving = resident_alive[None, :] & (home_dev[None, :] == sources)
    rank_table = jnp.cumsum(arriving.astype(jnp.int32), axis=1) - 1
    arrive_rank = jnp.sum(jnp.where(arriving, rank_table, 0), axis=0)
    recv_index = jnp.where(resident_alive, home_dev * capacity + arrive_rank, 0)

    row_tables = angle_tables(jnp.arange(rows_per_block, dtype=jnp.int32), head_dim)
    base_tables = angle_tables(block_numbers * rows_per_block, head_dim)
    tables = (*row_tables, *base_tables)
    token_ids = jnp.arange(turn_len, dtype=jnp.int32)
    order = jnp.arange(tp_count, dtype=jnp.int32) ^ tp_index

    outputs = []
    for seat in range(per_owner):
        cosine, sine = angle_tables(own_lengths[seat] + token_ids, head_dim)
        rows = slice(seat * turn_len, (seat + 1) * turn_len)
        queries = turn_query[rows].astype(jnp.float32).reshape(turn_len, group_size, head_dim)
        queries = queries * cosine[:, None, :] + rotate_halves(queries) * sine[:, None, :]
        queries = jnp.transpose(queries.astype(jnp.bfloat16), (1, 0, 2))
        new_keys = turn_key[rows].astype(jnp.float32)
        new_keys = (new_keys * cosine + rotate_halves(new_keys) * sine).astype(jnp.bfloat16)
        attended = attend(
            seat, recv_index, own_lengths, queries, new_keys, turn_value[rows], tables, arrived
        )
        outputs.append(lax.all_gather(attended, "tp", axis=0, tiled=False))
    return jnp.concatenate([project(order, gathered, weights) for gathered in outputs], axis=0)


def solution(mesh):
    return jax.shard_map(
        local,
        mesh=mesh,
        in_specs=(
            P("pool", "tp"),
            P("pool", "tp"),
            P("pool", "tp"),
            P("pool", None, "tp"),
            P("pool", None, "tp"),
            P(),
            P(),
            P(),
            P("tp", "pool"),
        ),
        out_specs=P("pool", "tp"),
        check_vma=False,
    )
```

```python
import functools
import math

import jax
import jax.numpy as jnp
import numpy as np
from jax import lax
from jax.experimental import pallas as pl
from jax.experimental.pallas import tpu as pltpu
from jax.sharding import PartitionSpec as P

rope_base = 1000000.0
CHUNK_BLOCKS = 16
MIB = 1024 * 1024
PROJ_MIB = 24
ATT_MIB = 2
ATT_VMEM = 32
EARLY_PIECES = 5
VMEM = pl.BlockSpec(memory_space=pltpu.VMEM)
SMEM = pl.BlockSpec(memory_space=pltpu.SMEM)
ANY = pl.BlockSpec(memory_space=pl.ANY)


def angle_tables(positions, head_dim):
    half_dim = head_dim // 2
    inverse = rope_base ** (-2.0 * np.arange(half_dim) / head_dim)
    angles = positions[:, None] * inverse[None, :]
    cosine, sine = np.cos(angles), np.sin(angles)
    return (
        np.concatenate([cosine, cosine], axis=1).astype(np.float32),
        np.concatenate([-sine, sine], axis=1).astype(np.float32),
    )


def add_angles(cos_a, sin_a, cos_b, sin_b):
    return cos_a * cos_b - sin_a * sin_b, sin_a * cos_b + cos_a * sin_b


def rope(values, cosine, sine):
    return values * cosine + pltpu.roll(values, values.shape[-1] // 2, 1) * sine


def table_rows(block_rows, base_count):
    return (
        slice(0, block_rows),
        slice(block_rows, 2 * block_rows),
        2 * block_rows,
        2 * block_rows + base_count,
    )


def send_kernel(
    base_count,
    place_ref,
    seats_ref,
    lengths_ref,
    map_ref,
    table_ref,
    keys_ref,
    vals_ref,
    out_ref,
    held,
    tables,
    plan,
    plan_scalar,
    in_sems,
    out_sems,
    other_sems,
):
    count = held.shape[0]
    blocks_here, block_rows = keys_ref.shape[:2]
    block_count, sessions = map_ref.shape
    shift = blocks_here.bit_length() - 1
    lanes = plan.shape[1]
    get_tables = pltpu.make_async_copy(table_ref, tables, other_sems.at[0])
    get_tables.start()

    lengths = lengths_ref[...].astype(jnp.float32)
    block = lax.broadcasted_iota(jnp.int32, (block_count, sessions), 0)
    here = ((block * block_rows).astype(jnp.float32) < lengths) & (
        map_ref[...] >> shift == place_ref[0]
    )
    code = (block * blocks_here + (map_ref[...] & (blocks_here - 1))).astype(jnp.float32)
    lowest = jnp.min(jnp.where(here, code, 1e6), axis=0, keepdims=True)
    highest = jnp.max(jnp.where(here, code, -1.0), axis=0, keepdims=True)
    number = jnp.sum(jnp.where(here, 1.0, 0.0), axis=0, keepdims=True)

    seat_row = seats_ref[...].astype(jnp.float32)
    down = lax.broadcasted_iota(jnp.int32, (sessions, sessions), 0)
    along = lax.broadcasted_iota(jnp.int32, (sessions, sessions), 1)
    seat_column = jnp.sum(jnp.where(down == along, seat_row, 0.0), axis=1, keepdims=True)
    seated = seat_column == along.astype(jnp.float32)
    down = lax.broadcasted_iota(jnp.int32, (sessions, lanes), 0)
    along = lax.broadcasted_iota(jnp.int32, (sessions, lanes), 1)

    def by_seat(row):
        column = jnp.sum(jnp.where(seated, row, 0.0), axis=1, keepdims=True)
        return jnp.sum(jnp.where(down == along, column, 0.0), axis=0, keepdims=True)

    low, high, num = by_seat(lowest), by_seat(highest), by_seat(number)
    low_next, high_next, num_next = (pltpu.roll(x, lanes - 1, 1) for x in (low, high, num))
    first = jnp.where(num >= 1.0, low, jnp.where(num_next >= 1.0, low_next, -1.0))
    second = jnp.where(
        num >= 2.0,
        high,
        jnp.where(
            num >= 1.0,
            jnp.where(num_next >= 1.0, low_next, -1.0),
            jnp.where(num_next >= 2.0, high_next, -1.0),
        ),
    )
    even = lax.broadcasted_iota(jnp.int32, (1, lanes), 1) % 2 == 0
    plan[...] = jnp.where(even, first, pltpu.roll(second, 1, 1)).astype(jnp.int32)
    to_scalar = pltpu.make_async_copy(plan, plan_scalar, other_sems.at[1])
    to_scalar.start()
    to_scalar.wait()

    @pl.loop(0, count)
    def _(i):
        code = plan_scalar[0, i]

        @pl.when(code >= 0)
        def _():
            slot = code & (blocks_here - 1)
            pltpu.make_async_copy(keys_ref.at[slot], held.at[i, 0], in_sems.at[i]).start()
            pltpu.make_async_copy(vals_ref.at[slot], held.at[i, 1], in_sems.at[i]).start()

    get_tables.wait()
    row_cos, row_sin, base_cos, base_sin = table_rows(block_rows, base_count)

    @pl.loop(0, count)
    def _(i):
        code = plan_scalar[0, i]

        @pl.when(code >= 0)
        def _():
            pltpu.make_async_copy(held.at[i], held.at[i], in_sems.at[i]).wait()
            position = code >> shift
            cosine, sine = add_angles(
                tables[row_cos, :],
                tables[row_sin, :],
                tables[pl.ds(base_cos + position, 1), :],
                tables[pl.ds(base_sin + position, 1), :],
            )
            held[i, 0] = rope(held[i, 0].astype(jnp.float32), cosine, sine).astype(jnp.bfloat16)
            pltpu.make_async_copy(held.at[i], out_ref.at[i], out_sems.at[i]).start()

    @pl.loop(0, count)
    def _(i):
        @pl.when(plan_scalar[0, i] >= 0)
        def _():
            pltpu.make_async_copy(held.at[i], out_ref.at[i], out_sems.at[i]).wait()


def send_blocks(place, seats, lengths, map_t, table, base_count, pool_keys, pool_values, count):
    block_shape = pool_keys.shape[1:]
    return pl.pallas_call(
        functools.partial(send_kernel, base_count),
        out_shape=jax.ShapeDtypeStruct((count, 2) + block_shape, pool_keys.dtype),
        in_specs=[SMEM] + [VMEM] * 3 + [ANY] * 3,
        out_specs=ANY,
        scratch_shapes=[
            pltpu.VMEM((count, 2) + block_shape, pool_keys.dtype),
            pltpu.VMEM(table.shape, jnp.float32),
            pltpu.VMEM((1, 128), jnp.int32),
            pltpu.SMEM((1, 128), jnp.int32),
            pltpu.SemaphoreType.DMA((count,)),
            pltpu.SemaphoreType.DMA((count,)),
            pltpu.SemaphoreType.DMA((2,)),
        ],
        compiler_params=pltpu.CompilerParams(vmem_limit_bytes=60 * MIB),
        name="send_blocks",
    )(place, seats[None, :], lengths[None, :], map_t, table, pool_keys, pool_values)


def prepare_kernel(
    place_ref,
    seats_ref,
    lengths_ref,
    map_ref,
    tables,
    query_ref,
    key_ref,
    index_ref,
    own_ref,
    out_query_ref,
    out_key_ref,
    counts,
    *,
    base_count,
    blocks_here,
    capacity,
    block_rows,
):
    per_owner, heads, turn_len, head_dim = out_query_ref.shape
    block_count = index_ref.shape[1]
    shift = blocks_here.bit_length() - 1
    row_shift = block_rows.bit_length() - 1
    scaling = math.log2(math.e) / math.sqrt(head_dim)
    row_cos, row_sin, base_cos, base_sin = table_rows(block_rows, base_count)

    @pl.loop(0, counts.shape[0])
    def _(i):
        counts[i] = 0

    for seat in range(per_owner):
        session = seats_ref[place_ref[0] * per_owner + seat]
        length = lengths_ref[session]
        own_ref[seat] = length
        live = pl.cdiv(length, block_rows)

        @pl.loop(0, live)
        def _(j):
            source = map_ref[j, session] >> shift
            rank = counts[source]
            counts[source] = rank + 1
            index_ref[seat, j] = source * capacity + rank

        @pl.loop(live, block_count)
        def _(j):
            index_ref[seat, j] = index_ref[seat, 0]

        near = length & (block_rows - 1)
        far = length >> row_shift
        start_cos, start_sin = add_angles(
            tables[pl.ds(near, 1), :],
            tables[pl.ds(block_rows + near, 1), :],
            tables[pl.ds(base_cos + far, 1), :],
            tables[pl.ds(base_sin + far, 1), :],
        )
        for part in range(turn_len // block_rows):
            part_cos, part_sin = add_angles(
                start_cos,
                start_sin,
                tables[base_cos + part : base_cos + part + 1, :],
                tables[base_sin + part : base_sin + part + 1, :],
            )
            cosine, sine = add_angles(tables[row_cos, :], tables[row_sin, :], part_cos, part_sin)
            here = slice(part * block_rows, (part + 1) * block_rows)
            rows = slice(seat * turn_len + here.start, seat * turn_len + here.stop)
            key = key_ref[rows, :].astype(jnp.float32)
            out_key_ref[seat, here, :] = rope(key, cosine, sine).astype(jnp.bfloat16)
            cosine, sine = cosine * scaling, sine * scaling
            for h in range(heads):
                query = query_ref[rows, h * head_dim : (h + 1) * head_dim].astype(jnp.float32)
                out_query_ref[seat, h, here, :] = rope(query, cosine, sine).astype(jnp.bfloat16)


def prepare_turn(place, seats, lengths, map_t, table, base_count, turn_query, turn_key, sizes):
    pooled_count, blocks_here, capacity, per_owner, block_rows, head_dim = sizes
    turn_len = turn_query.shape[0] // per_owner
    heads = turn_query.shape[1] // head_dim
    block_count = map_t.shape[0]
    return pl.pallas_call(
        functools.partial(
            prepare_kernel,
            base_count=base_count,
            blocks_here=blocks_here,
            capacity=capacity,
            block_rows=block_rows,
        ),
        out_shape=(
            jax.ShapeDtypeStruct((per_owner, block_count), jnp.int32),
            jax.ShapeDtypeStruct((per_owner,), jnp.int32),
            jax.ShapeDtypeStruct((per_owner, heads, turn_len, head_dim), jnp.bfloat16),
            jax.ShapeDtypeStruct((per_owner, turn_len, head_dim), jnp.bfloat16),
        ),
        in_specs=[SMEM] * 4 + [VMEM] * 3,
        out_specs=(SMEM, SMEM, VMEM, VMEM),
        scratch_shapes=[pltpu.SMEM((pooled_count,), jnp.int32)],
        compiler_params=pltpu.CompilerParams(vmem_limit_bytes=16 * MIB),
        name="prepare_turn",
    )(place, seats, lengths, map_t, table, turn_query, turn_key)


def attention_kernel(
    seat,
    index_ref,
    length_ref,
    query_ref,
    turn_key_ref,
    turn_val_ref,
    arrived_ref,
    out_ref,
    blocks,
    top_ref,
    acc_ref,
    sems,
):
    _, heads, turn_len, head_dim = query_ref.shape
    _, _, block_rows, _ = blocks.shape
    chunk_rows = CHUNK_BLOCKS * block_rows
    length = length_ref[seat]
    chunks = pl.cdiv(length, chunk_rows)
    full = length // chunk_rows

    def copy(j):
        return pltpu.make_async_copy(arrived_ref.at[index_ref[seat, j]], blocks.at[j], sems.at[j])

    @pl.loop(0, chunks * CHUNK_BLOCKS, step=4)
    def _(j):
        for i in range(4):
            copy(j + i).start()

    def scores(h, keys):
        return lax.dot_general(
            query_ref[seat, h], keys, (((1,), (1,)), ((), ())), preferred_element_type=jnp.float32
        )

    def with_ones(vals):
        return jnp.concatenate([vals, jnp.ones(vals.shape, vals.dtype)], axis=1)

    rows = lax.broadcasted_iota(jnp.int32, (turn_len, turn_len), 0)
    cols = lax.broadcasted_iota(jnp.int32, (turn_len, turn_len), 1)
    new_keys = turn_key_ref[seat]
    new_vals = with_ones(turn_val_ref[seat * turn_len : (seat + 1) * turn_len, :])
    seen = [jnp.where(cols <= rows, scores(h, new_keys), -jnp.inf) for h in range(heads)]
    for h in range(heads):
        top = jnp.max(seen[h], axis=1, keepdims=True)
        weight = jnp.exp2(seen[h] - top).astype(jnp.bfloat16)
        top_ref[h] = top
        acc_ref[h] = jnp.dot(weight, new_vals, preferred_element_type=jnp.float32)

    def chunk_step(c, masked):
        first = c * CHUNK_BLOCKS

        @pl.loop(0, CHUNK_BLOCKS, step=4)
        def _(j):
            for i in range(4):
                copy(first + j + i).wait()

        keys = blocks[pl.ds(first, CHUNK_BLOCKS), 0].reshape(chunk_rows, head_dim)
        vals = with_ones(blocks[pl.ds(first, CHUNK_BLOCKS), 1].reshape(chunk_rows, head_dim))
        seen = [scores(h, keys) for h in range(heads)]
        if masked:
            place = c * chunk_rows + lax.broadcasted_iota(jnp.int32, seen[0].shape, 1)
            seen = [jnp.where(place < length, s, -jnp.inf) for s in seen]
        for h in range(heads):
            old = top_ref[h]
            top = jnp.maximum(old, jnp.max(seen[h], axis=1, keepdims=True))
            weight = jnp.exp2(seen[h] - top).astype(jnp.bfloat16)
            fade = jnp.exp2(old - top)
            top_ref[h] = top
            acc_ref[h] = acc_ref[h] * fade + jnp.dot(
                weight, vals, preferred_element_type=jnp.float32
            )

    @pl.loop(0, full)
    def _(c):
        chunk_step(c, False)

    @pl.when(full < chunks)
    def _():
        chunk_step(full, True)

    for h in range(heads):
        acc = acc_ref[h]
        out_ref[:, h * head_dim : (h + 1) * head_dim] = (
            acc[:, :head_dim] / acc[:, head_dim:]
        ).astype(jnp.bfloat16)


def attend(seat, recv_index, lengths, query, turn_key, turn_val, arrived):
    _, heads, turn_len, head_dim = query.shape
    block_rows = arrived.shape[2]
    block_count = recv_index.shape[1]
    keys_seen = block_count * block_rows + turn_len
    return pl.pallas_call(
        functools.partial(attention_kernel, seat),
        out_shape=jax.ShapeDtypeStruct((turn_len, heads * head_dim), jnp.bfloat16),
        in_specs=[SMEM] * 2 + [VMEM] * 3 + [ANY],
        out_specs=VMEM,
        scratch_shapes=[
            pltpu.VMEM((block_count, 2, block_rows, head_dim), jnp.bfloat16),
            pltpu.VMEM((heads, turn_len, 1), jnp.float32),
            pltpu.VMEM((heads, turn_len, 2 * head_dim), jnp.float32),
            pltpu.SemaphoreType.DMA((block_count,)),
        ],
        compiler_params=pltpu.CompilerParams(vmem_limit_bytes=ATT_VMEM * MIB),
        cost_estimate=pl.CostEstimate(
            flops=4 * heads * turn_len * keys_seen * head_dim,
            bytes_accessed=ATT_MIB * MIB,
            transcendentals=heads * turn_len * keys_seen,
        ),
        name="attend",
    )(recv_index, lengths, query, turn_key, turn_val, arrived)


def project_kernel(distances, started, place_ref, *refs):
    row_refs, refs = refs[:-5], refs[-5:]
    if started:
        row_refs, before_ref = row_refs[:-1], row_refs[-1]
    weight_ref, out_ref, held, rows, sems = refs
    pieces, _, width = held.shape
    depth = weight_ref.shape[1]
    count = len(distances)
    turn_len = row_refs[0].shape[0]
    tp = place_ref[0]
    groups = weight_ref.shape[0] // pieces

    def copy(i, j):
        home = weight_place(tp, (tp - distances[i]) & (groups - 1), j, pieces)
        return pltpu.make_async_copy(
            weight_ref.at[home], held.at[j, i * depth : (i + 1) * depth], sems.at[i, j]
        )

    for j in range(pieces):
        for i in range(count):
            copy(i, j).start()
    for k, row_ref in enumerate(row_refs):
        seat, i = divmod(k, count)
        rows[seat * turn_len : (seat + 1) * turn_len, i * depth : (i + 1) * depth] = row_ref[...]
    for j in range(pieces):
        for i in range(count):
            copy(i, j).wait()
        cols = slice(j * width, (j + 1) * width)
        for first in range(0, rows.shape[0], turn_len):
            here = slice(first, first + turn_len)
            part = jnp.dot(rows[here], held[j], preferred_element_type=jnp.float32)
            if started:
                part = part + before_ref[here, cols]
            out_ref[here, cols] = part.astype(out_ref.dtype)


def project(place, distances, gathered, before, weights, pieces, out_type):
    count = len(gathered[0])
    rows, depth = gathered[0][0].shape
    width = weights.shape[2]
    flat = [piece for seat in gathered for piece in seat]
    flat = flat if before is None else flat + [before]
    return pl.pallas_call(
        functools.partial(project_kernel, distances, before is not None),
        out_shape=jax.ShapeDtypeStruct((rows * len(gathered), pieces * width), out_type),
        in_specs=[SMEM] + [VMEM] * len(flat) + [pl.BlockSpec(memory_space=pltpu.HBM)],
        out_specs=VMEM,
        scratch_shapes=[
            pltpu.VMEM((pieces, count * depth, width), jnp.bfloat16),
            pltpu.VMEM((rows * len(gathered), count * depth), jnp.bfloat16),
            pltpu.SemaphoreType.DMA((count, pieces)),
        ],
        compiler_params=pltpu.CompilerParams(vmem_limit_bytes=PROJ_MIB * MIB),
        cost_estimate=pl.CostEstimate(
            flops=2 * rows * len(gathered) * count * depth * pieces * width,
            bytes_accessed=8 * MIB,
            transcendentals=0,
        ),
        name="project",
    )(place, *flat, weights)


def weight_place(plane, tp, rest, pieces):
    return (plane ^ tp) * pieces + rest


def spread_weights(out_weight, pieces):
    moves = []
    for p in range(lax.axis_size("pool")):
        for t in range(lax.axis_size("tp")):
            to = weight_place(p // pieces, t, p % pieces, pieces)
            moves.append((p * lax.axis_size("tp") + t, to * lax.axis_size("tp") + t))
    return lax.ppermute(out_weight, ("pool", "tp"), moves)


def to_planes(values, pieces):
    moves = []
    for p in range(lax.axis_size("pool")):
        for t in range(lax.axis_size("tp")):
            to = weight_place(p // pieces, t, p % pieces, pieces)
            moves.append((to * lax.axis_size("tp") + t, to * lax.axis_size("tp") + p // pieces))
    return lax.ppermute(values, ("pool", "tp"), moves)


def shift_tp(values, step):
    count = lax.axis_size("tp")
    return lax.ppermute(values, "tp", [(i, (i + step) % count) for i in range(count)])


def gather_ring(piece, farthest_from_left):
    count = lax.axis_size("tp")
    pieces, distances = [piece], [0]
    from_left = from_right = piece
    for distance in range(1, count // 2 + 1):
        last = 2 * distance == count
        if not last or farthest_from_left:
            from_left = shift_tp(from_left, 1)
            pieces.append(from_left)
            distances.append(distance)
        if not last or not farthest_from_left:
            from_right = shift_tp(from_right, -1)
            pieces.append(from_right)
            distances.append(-distance)
    return pieces, distances


def local(
    turn_query,
    turn_key,
    turn_value,
    pool_keys,
    pool_values,
    seat_session,
    history_len,
    block_map,
    out_weight,
):
    pooled_count = lax.axis_size("pool")
    tp_count = lax.axis_size("tp")
    place = lax.axis_index("pool")[None]
    blocks_here, rows_per_block, head_dim = pool_keys.shape
    block_count = block_map.shape[1]
    per_owner = seat_session.shape[0] // pooled_count
    capacity = per_owner * block_count // pooled_count
    pieces = pooled_count // tp_count

    base_count = block_count + 8
    table = jnp.asarray(
        np.concatenate(
            [
                *angle_tables(np.arange(rows_per_block), head_dim),
                *angle_tables(np.arange(base_count) * rows_per_block, head_dim),
            ]
        )
    )
    map_t = block_map.T

    spread = spread_weights(out_weight, pieces)
    sent = send_blocks(
        place,
        seat_session,
        history_len,
        map_t,
        table,
        base_count,
        pool_keys,
        pool_values,
        pooled_count * capacity,
    )
    sent, spread = lax.optimization_barrier((sent, spread))
    arrived = lax.all_to_all(sent, "pool", split_axis=0, concat_axis=0, tiled=True)

    turn_query, turn_key, _ = lax.optimization_barrier((turn_query, turn_key, sent))
    sizes = (pooled_count, blocks_here, capacity, per_owner, rows_per_block, head_dim)
    recv_index, own_lengths, queries, new_keys = prepare_turn(
        place, seat_session, history_len, map_t, table, base_count, turn_query, turn_key, sizes
    )
    moved = to_planes(spread, pieces)
    weights = lax.all_gather(moved, "pool", axis=0, tiled=False)

    gathered = []
    for seat in range(per_owner):
        attended = attend(seat, recv_index, own_lengths, queries, new_keys, turn_value, arrived)
        if gathered:
            attended, *_ = lax.optimization_barrier((attended, *gathered[-1][1:3]))
        ring, distances = gather_ring(attended, seat % 2 == 0)
        gathered.append(ring)
    early = EARLY_PIECES
    where = lax.axis_index("tp")[None]
    near, far = ([ring[:early] for ring in gathered], [ring[early:] for ring in gathered])
    partial = project(where, distances[:early], near, None, weights, pieces, jnp.float32)
    return project(where, distances[early:], far, partial, weights, pieces, jnp.bfloat16)


def solution(mesh):
    return jax.shard_map(
        local,
        mesh=mesh,
        in_specs=(
            P("pool", "tp"),
            P("pool", "tp"),
            P("pool", "tp"),
            P("pool", None, "tp"),
            P("pool", None, "tp"),
            P(),
            P(),
            P(),
            P("tp", "pool"),
        ),
        out_specs=P("pool", "tp"),
        check_vma=False,
    )
```

```python
import functools
import math

import jax
import jax.numpy as jnp
import numpy as np
from jax import lax
from jax.experimental import pallas as pl
from jax.experimental.pallas import tpu as pltpu
from jax.sharding import PartitionSpec as P

rope_base = 1000000.0
CHUNK_BLOCKS = 16
MIB = 1024 * 1024
PROJ_MIB = 52
ATT_MIB = 2
ATT_VMEM = 32
EARLY_PIECES = 0
VMEM = pl.BlockSpec(memory_space=pltpu.VMEM)
SMEM = pl.BlockSpec(memory_space=pltpu.SMEM)
ANY = pl.BlockSpec(memory_space=pl.ANY)


def angle_tables(positions, head_dim):
    half_dim = head_dim // 2
    inverse = rope_base ** (-2.0 * np.arange(half_dim) / head_dim)
    angles = positions[:, None] * inverse[None, :]
    cosine, sine = np.cos(angles), np.sin(angles)
    return (
        np.concatenate([cosine, cosine], axis=1).astype(np.float32),
        np.concatenate([-sine, sine], axis=1).astype(np.float32),
    )


def add_angles(cos_a, sin_a, cos_b, sin_b):
    return cos_a * cos_b - sin_a * sin_b, sin_a * cos_b + cos_a * sin_b


def rope(values, cosine, sine):
    return values * cosine + pltpu.roll(values, values.shape[-1] // 2, 1) * sine


def table_rows(block_rows, base_count):
    return (
        slice(0, block_rows),
        slice(block_rows, 2 * block_rows),
        2 * block_rows,
        2 * block_rows + base_count,
    )


def send_kernel(
    base_count,
    place_ref,
    seats_ref,
    lengths_ref,
    map_ref,
    table_ref,
    keys_ref,
    vals_ref,
    out_ref,
    held,
    tables,
    plan,
    plan_scalar,
    in_sems,
    out_sems,
    other_sems,
):
    count = held.shape[0]
    blocks_here, block_rows = keys_ref.shape[:2]
    block_count, sessions = map_ref.shape
    shift = blocks_here.bit_length() - 1
    lanes = plan.shape[1]
    get_tables = pltpu.make_async_copy(table_ref, tables, other_sems.at[0])
    get_tables.start()

    lengths = lengths_ref[...].astype(jnp.float32)
    block = lax.broadcasted_iota(jnp.int32, (block_count, sessions), 0)
    here = ((block * block_rows).astype(jnp.float32) < lengths) & (
        map_ref[...] >> shift == place_ref[0]
    )
    code = (block * blocks_here + (map_ref[...] & (blocks_here - 1))).astype(jnp.float32)
    lowest = jnp.min(jnp.where(here, code, 1e6), axis=0, keepdims=True)
    highest = jnp.max(jnp.where(here, code, -1.0), axis=0, keepdims=True)
    number = jnp.sum(jnp.where(here, 1.0, 0.0), axis=0, keepdims=True)

    seat_row = seats_ref[...].astype(jnp.float32)
    down = lax.broadcasted_iota(jnp.int32, (sessions, sessions), 0)
    along = lax.broadcasted_iota(jnp.int32, (sessions, sessions), 1)
    seat_column = jnp.sum(jnp.where(down == along, seat_row, 0.0), axis=1, keepdims=True)
    seated = seat_column == along.astype(jnp.float32)
    down = lax.broadcasted_iota(jnp.int32, (sessions, lanes), 0)
    along = lax.broadcasted_iota(jnp.int32, (sessions, lanes), 1)

    def by_seat(row):
        column = jnp.sum(jnp.where(seated, row, 0.0), axis=1, keepdims=True)
        return jnp.sum(jnp.where(down == along, column, 0.0), axis=0, keepdims=True)

    low, high, num = by_seat(lowest), by_seat(highest), by_seat(number)
    low_next, high_next, num_next = (pltpu.roll(x, lanes - 1, 1) for x in (low, high, num))
    first = jnp.where(num >= 1.0, low, jnp.where(num_next >= 1.0, low_next, -1.0))
    second = jnp.where(
        num >= 2.0,
        high,
        jnp.where(
            num >= 1.0,
            jnp.where(num_next >= 1.0, low_next, -1.0),
            jnp.where(num_next >= 2.0, high_next, -1.0),
        ),
    )
    even = lax.broadcasted_iota(jnp.int32, (1, lanes), 1) % 2 == 0
    plan[...] = jnp.where(even, first, pltpu.roll(second, 1, 1)).astype(jnp.int32)
    to_scalar = pltpu.make_async_copy(plan, plan_scalar, other_sems.at[1])
    to_scalar.start()
    to_scalar.wait()

    @pl.loop(0, count)
    def _(i):
        code = plan_scalar[0, i]

        @pl.when(code >= 0)
        def _():
            slot = code & (blocks_here - 1)
            pltpu.make_async_copy(keys_ref.at[slot], held.at[i, 0], in_sems.at[i]).start()
            pltpu.make_async_copy(vals_ref.at[slot], held.at[i, 1], in_sems.at[i]).start()

    get_tables.wait()
    row_cos, row_sin, base_cos, base_sin = table_rows(block_rows, base_count)

    @pl.loop(0, count)
    def _(i):
        code = plan_scalar[0, i]

        @pl.when(code >= 0)
        def _():
            pltpu.make_async_copy(held.at[i], held.at[i], in_sems.at[i]).wait()
            position = code >> shift
            cosine, sine = add_angles(
                tables[row_cos, :],
                tables[row_sin, :],
                tables[pl.ds(base_cos + position, 1), :],
                tables[pl.ds(base_sin + position, 1), :],
            )
            held[i, 0] = rope(held[i, 0].astype(jnp.float32), cosine, sine).astype(jnp.bfloat16)
            pltpu.make_async_copy(held.at[i], out_ref.at[i], out_sems.at[i]).start()

    @pl.loop(0, count)
    def _(i):
        @pl.when(plan_scalar[0, i] >= 0)
        def _():
            pltpu.make_async_copy(held.at[i], out_ref.at[i], out_sems.at[i]).wait()


def send_blocks(place, seats, lengths, map_t, table, base_count, pool_keys, pool_values, count):
    block_shape = pool_keys.shape[1:]
    return pl.pallas_call(
        functools.partial(send_kernel, base_count),
        out_shape=jax.ShapeDtypeStruct((count, 2) + block_shape, pool_keys.dtype),
        in_specs=[SMEM] + [VMEM] * 3 + [ANY] * 3,
        out_specs=ANY,
        scratch_shapes=[
            pltpu.VMEM((count, 2) + block_shape, pool_keys.dtype),
            pltpu.VMEM(table.shape, jnp.float32),
            pltpu.VMEM((1, 128), jnp.int32),
            pltpu.SMEM((1, 128), jnp.int32),
            pltpu.SemaphoreType.DMA((count,)),
            pltpu.SemaphoreType.DMA((count,)),
            pltpu.SemaphoreType.DMA((2,)),
        ],
        compiler_params=pltpu.CompilerParams(vmem_limit_bytes=60 * MIB),
        name="send_blocks",
    )(place, seats[None, :], lengths[None, :], map_t, table, pool_keys, pool_values)


def prepare_kernel(
    place_ref,
    seats_ref,
    lengths_ref,
    map_ref,
    tables,
    query_ref,
    key_ref,
    index_ref,
    own_ref,
    out_query_ref,
    out_key_ref,
    counts,
    *,
    base_count,
    blocks_here,
    capacity,
    block_rows,
):
    per_owner, heads, turn_len, head_dim = out_query_ref.shape
    block_count = index_ref.shape[1]
    shift = blocks_here.bit_length() - 1
    row_shift = block_rows.bit_length() - 1
    scaling = math.log2(math.e) / math.sqrt(head_dim)
    row_cos, row_sin, base_cos, base_sin = table_rows(block_rows, base_count)

    @pl.loop(0, counts.shape[0])
    def _(i):
        counts[i] = 0

    for seat in range(per_owner):
        session = seats_ref[place_ref[0] * per_owner + seat]
        length = lengths_ref[session]
        own_ref[seat] = length
        live = pl.cdiv(length, block_rows)

        @pl.loop(0, live)
        def _(j):
            source = map_ref[j, session] >> shift
            rank = counts[source]
            counts[source] = rank + 1
            index_ref[seat, j] = source * capacity + rank

        @pl.loop(live, block_count)
        def _(j):
            index_ref[seat, j] = index_ref[seat, 0]

        near = length & (block_rows - 1)
        far = length >> row_shift
        start_cos, start_sin = add_angles(
            tables[pl.ds(near, 1), :],
            tables[pl.ds(block_rows + near, 1), :],
            tables[pl.ds(base_cos + far, 1), :],
            tables[pl.ds(base_sin + far, 1), :],
        )
        for part in range(turn_len // block_rows):
            part_cos, part_sin = add_angles(
                start_cos,
                start_sin,
                tables[base_cos + part : base_cos + part + 1, :],
                tables[base_sin + part : base_sin + part + 1, :],
            )
            cosine, sine = add_angles(tables[row_cos, :], tables[row_sin, :], part_cos, part_sin)
            here = slice(part * block_rows, (part + 1) * block_rows)
            rows = slice(seat * turn_len + here.start, seat * turn_len + here.stop)
            key = key_ref[rows, :].astype(jnp.float32)
            out_key_ref[seat, here, :] = rope(key, cosine, sine).astype(jnp.bfloat16)
            cosine, sine = cosine * scaling, sine * scaling
            for h in range(heads):
                query = query_ref[rows, h * head_dim : (h + 1) * head_dim].astype(jnp.float32)
                out_query_ref[seat, h, here, :] = rope(query, cosine, sine).astype(jnp.bfloat16)


def prepare_turn(place, seats, lengths, map_t, table, base_count, turn_query, turn_key, sizes):
    pooled_count, blocks_here, capacity, per_owner, block_rows, head_dim = sizes
    turn_len = turn_query.shape[0] // per_owner
    heads = turn_query.shape[1] // head_dim
    block_count = map_t.shape[0]
    return pl.pallas_call(
        functools.partial(
            prepare_kernel,
            base_count=base_count,
            blocks_here=blocks_here,
            capacity=capacity,
            block_rows=block_rows,
        ),
        out_shape=(
            jax.ShapeDtypeStruct((per_owner, block_count), jnp.int32),
            jax.ShapeDtypeStruct((per_owner,), jnp.int32),
            jax.ShapeDtypeStruct((per_owner, heads, turn_len, head_dim), jnp.bfloat16),
            jax.ShapeDtypeStruct((per_owner, turn_len, head_dim), jnp.bfloat16),
        ),
        in_specs=[SMEM] * 4 + [VMEM] * 3,
        out_specs=(SMEM, SMEM, VMEM, VMEM),
        scratch_shapes=[pltpu.SMEM((pooled_count,), jnp.int32)],
        compiler_params=pltpu.CompilerParams(vmem_limit_bytes=16 * MIB),
        name="prepare_turn",
    )(place, seats, lengths, map_t, table, turn_query, turn_key)


def attention_kernel(
    seat,
    index_ref,
    length_ref,
    query_ref,
    turn_key_ref,
    turn_val_ref,
    arrived_ref,
    out_ref,
    blocks,
    top_ref,
    acc_ref,
    sems,
):
    _, heads, turn_len, head_dim = query_ref.shape
    _, _, block_rows, _ = blocks.shape
    chunk_rows = CHUNK_BLOCKS * block_rows
    length = length_ref[seat]
    chunks = pl.cdiv(length, chunk_rows)
    full = length // chunk_rows

    def copy(j):
        return pltpu.make_async_copy(arrived_ref.at[index_ref[seat, j]], blocks.at[j], sems.at[j])

    @pl.loop(0, chunks * CHUNK_BLOCKS, step=4)
    def _(j):
        for i in range(4):
            copy(j + i).start()

    def scores(h, keys):
        return lax.dot_general(
            query_ref[seat, h], keys, (((1,), (1,)), ((), ())), preferred_element_type=jnp.float32
        )

    def with_ones(vals):
        return jnp.concatenate([vals, jnp.ones(vals.shape, vals.dtype)], axis=1)

    rows = lax.broadcasted_iota(jnp.int32, (turn_len, turn_len), 0)
    cols = lax.broadcasted_iota(jnp.int32, (turn_len, turn_len), 1)
    new_keys = turn_key_ref[seat]
    new_vals = with_ones(turn_val_ref[seat * turn_len : (seat + 1) * turn_len, :])
    seen = [jnp.where(cols <= rows, scores(h, new_keys), -jnp.inf) for h in range(heads)]
    for h in range(heads):
        top = jnp.max(seen[h], axis=1, keepdims=True)
        weight = jnp.exp2(seen[h] - top).astype(jnp.bfloat16)
        top_ref[h] = top
        acc_ref[h] = jnp.dot(weight, new_vals, preferred_element_type=jnp.float32)

    def chunk_step(c, masked):
        first = c * CHUNK_BLOCKS

        @pl.loop(0, CHUNK_BLOCKS, step=4)
        def _(j):
            for i in range(4):
                copy(first + j + i).wait()

        keys = blocks[pl.ds(first, CHUNK_BLOCKS), 0].reshape(chunk_rows, head_dim)
        vals = with_ones(blocks[pl.ds(first, CHUNK_BLOCKS), 1].reshape(chunk_rows, head_dim))
        seen = [scores(h, keys) for h in range(heads)]
        if masked:
            place = c * chunk_rows + lax.broadcasted_iota(jnp.int32, seen[0].shape, 1)
            seen = [jnp.where(place < length, s, -jnp.inf) for s in seen]
        for h in range(heads):
            old = top_ref[h]
            top = jnp.maximum(old, jnp.max(seen[h], axis=1, keepdims=True))
            weight = jnp.exp2(seen[h] - top).astype(jnp.bfloat16)
            fade = jnp.exp2(old - top)
            top_ref[h] = top
            acc_ref[h] = acc_ref[h] * fade + jnp.dot(
                weight, vals, preferred_element_type=jnp.float32
            )

    @pl.loop(0, full)
    def _(c):
        chunk_step(c, False)

    @pl.when(full < chunks)
    def _():
        chunk_step(full, True)

    for h in range(heads):
        acc = acc_ref[h]
        out_ref[:, h * head_dim : (h + 1) * head_dim] = (
            acc[:, :head_dim] / acc[:, head_dim:]
        ).astype(jnp.bfloat16)


def attend(seat, recv_index, lengths, query, turn_key, turn_val, arrived):
    _, heads, turn_len, head_dim = query.shape
    block_rows = arrived.shape[2]
    block_count = recv_index.shape[1]
    keys_seen = block_count * block_rows + turn_len
    return pl.pallas_call(
        functools.partial(attention_kernel, seat),
        out_shape=jax.ShapeDtypeStruct((turn_len, heads * head_dim), jnp.bfloat16),
        in_specs=[SMEM] * 2 + [VMEM] * 3 + [ANY],
        out_specs=VMEM,
        scratch_shapes=[
            pltpu.VMEM((block_count, 2, block_rows, head_dim), jnp.bfloat16),
            pltpu.VMEM((heads, turn_len, 1), jnp.float32),
            pltpu.VMEM((heads, turn_len, 2 * head_dim), jnp.float32),
            pltpu.SemaphoreType.DMA((block_count,)),
        ],
        compiler_params=pltpu.CompilerParams(vmem_limit_bytes=ATT_VMEM * MIB),
        cost_estimate=pl.CostEstimate(
            flops=4 * heads * turn_len * keys_seen * head_dim,
            bytes_accessed=ATT_MIB * MIB,
            transcendentals=heads * turn_len * keys_seen,
        ),
        name="attend",
    )(recv_index, lengths, query, turn_key, turn_val, arrived)


def project_kernel(distances, started, place_ref, *refs):
    row_refs, refs = refs[:-5], refs[-5:]
    if started:
        row_refs, before_ref = row_refs[:-1], row_refs[-1]
    weight_ref, out_ref, held, rows, sems = refs
    pieces, _, width = held.shape
    depth = weight_ref.shape[1]
    count = len(distances)
    turn_len = row_refs[0].shape[0]
    tp = place_ref[0]
    groups = weight_ref.shape[0] // pieces

    def copy(i, j):
        home = weight_place(tp, (tp - distances[i]) & (groups - 1), j, pieces)
        return pltpu.make_async_copy(
            weight_ref.at[home], held.at[j, i * depth : (i + 1) * depth], sems.at[i, j]
        )

    for j in range(pieces):
        for i in range(count):
            copy(i, j).start()
    for k, row_ref in enumerate(row_refs):
        seat, i = divmod(k, count)
        rows[seat * turn_len : (seat + 1) * turn_len, i * depth : (i + 1) * depth] = row_ref[...]
    for j in range(pieces):
        for i in range(count):
            copy(i, j).wait()
        cols = slice(j * width, (j + 1) * width)
        for first in range(0, rows.shape[0], turn_len):
            here = slice(first, first + turn_len)
            part = jnp.dot(rows[here], held[j], preferred_element_type=jnp.float32)
            if started:
                part = part + before_ref[here, cols]
            out_ref[here, cols] = part.astype(out_ref.dtype)


def project(place, distances, gathered, before, weights, pieces, out_type):
    count = len(gathered[0])
    rows, depth = gathered[0][0].shape
    width = weights.shape[2]
    flat = [piece for seat in gathered for piece in seat]
    flat = flat if before is None else flat + [before]
    return pl.pallas_call(
        functools.partial(project_kernel, distances, before is not None),
        out_shape=jax.ShapeDtypeStruct((rows * len(gathered), pieces * width), out_type),
        in_specs=[SMEM] + [VMEM] * len(flat) + [pl.BlockSpec(memory_space=pltpu.HBM)],
        out_specs=VMEM,
        scratch_shapes=[
            pltpu.VMEM((pieces, count * depth, width), jnp.bfloat16),
            pltpu.VMEM((rows * len(gathered), count * depth), jnp.bfloat16),
            pltpu.SemaphoreType.DMA((count, pieces)),
        ],
        compiler_params=pltpu.CompilerParams(vmem_limit_bytes=PROJ_MIB * MIB),
        cost_estimate=pl.CostEstimate(
            flops=2 * rows * len(gathered) * count * depth * pieces * width,
            bytes_accessed=8 * MIB,
            transcendentals=0,
        ),
        name="project",
    )(place, *flat, weights)


def weight_place(plane, tp, rest, pieces):
    return (plane ^ tp) * pieces + rest


def spread_weights(out_weight, pieces):
    moves = []
    for p in range(lax.axis_size("pool")):
        for t in range(lax.axis_size("tp")):
            to = weight_place(p // pieces, t, p % pieces, pieces)
            moves.append((p * lax.axis_size("tp") + t, to * lax.axis_size("tp") + t))
    return lax.ppermute(out_weight, ("pool", "tp"), moves)


def to_planes(values, pieces):
    moves = []
    for p in range(lax.axis_size("pool")):
        for t in range(lax.axis_size("tp")):
            to = weight_place(p // pieces, t, p % pieces, pieces)
            moves.append((to * lax.axis_size("tp") + t, to * lax.axis_size("tp") + p // pieces))
    return lax.ppermute(values, ("pool", "tp"), moves)


def shift_tp(values, step):
    count = lax.axis_size("tp")
    return lax.ppermute(values, "tp", [(i, (i + step) % count) for i in range(count)])


def gather_ring(piece, farthest_from_left):
    count = lax.axis_size("tp")
    pieces, distances = [piece], [0]
    from_left = from_right = piece
    for distance in range(1, count // 2 + 1):
        last = 2 * distance == count
        if not last or farthest_from_left:
            from_left = shift_tp(from_left, 1)
            pieces.append(from_left)
            distances.append(distance)
        if not last or not farthest_from_left:
            from_right = shift_tp(from_right, -1)
            pieces.append(from_right)
            distances.append(-distance)
    return pieces, distances


def local(
    turn_query,
    turn_key,
    turn_value,
    pool_keys,
    pool_values,
    seat_session,
    history_len,
    block_map,
    out_weight,
):
    pooled_count = lax.axis_size("pool")
    tp_count = lax.axis_size("tp")
    place = lax.axis_index("pool")[None]
    blocks_here, rows_per_block, head_dim = pool_keys.shape
    block_count = block_map.shape[1]
    per_owner = seat_session.shape[0] // pooled_count
    capacity = per_owner * block_count // pooled_count
    pieces = pooled_count // tp_count

    base_count = block_count + 8
    table = jnp.asarray(
        np.concatenate(
            [
                *angle_tables(np.arange(rows_per_block), head_dim),
                *angle_tables(np.arange(base_count) * rows_per_block, head_dim),
            ]
        )
    )
    map_t = block_map.T

    spread = spread_weights(out_weight, pieces)
    sent = send_blocks(
        place,
        seat_session,
        history_len,
        map_t,
        table,
        base_count,
        pool_keys,
        pool_values,
        pooled_count * capacity,
    )
    sent, spread = lax.optimization_barrier((sent, spread))
    arrived = lax.all_to_all(sent, "pool", split_axis=0, concat_axis=0, tiled=True)

    turn_query, turn_key, _ = lax.optimization_barrier((turn_query, turn_key, sent))
    sizes = (pooled_count, blocks_here, capacity, per_owner, rows_per_block, head_dim)
    recv_index, own_lengths, queries, new_keys = prepare_turn(
        place, seat_session, history_len, map_t, table, base_count, turn_query, turn_key, sizes
    )
    moved = to_planes(spread, pieces)
    moved, arrived, queries = lax.optimization_barrier((moved, arrived, queries))
    weights = lax.all_gather(moved, "pool", axis=0, tiled=False)

    gathered = []
    for seat in range(per_owner):
        attended = attend(seat, recv_index, own_lengths, queries, new_keys, turn_value, arrived)
        if gathered:
            attended, *_ = lax.optimization_barrier((attended, *gathered[-1][1:3]))
        ring, distances = gather_ring(attended, seat % 2 == 0)
        gathered.append(ring)
    early = EARLY_PIECES
    where = lax.axis_index("tp")[None]
    if early == 0:
        return project(where, distances, gathered, None, weights, pieces, jnp.bfloat16)
    near, far = ([ring[:early] for ring in gathered], [ring[early:] for ring in gathered])
    partial = project(where, distances[:early], near, None, weights, pieces, jnp.float32)
    return project(where, distances[early:], far, partial, weights, pieces, jnp.bfloat16)


def solution(mesh):
    return jax.shard_map(
        local,
        mesh=mesh,
        in_specs=(
            P("pool", "tp"),
            P("pool", "tp"),
            P("pool", "tp"),
            P("pool", None, "tp"),
            P("pool", None, "tp"),
            P(),
            P(),
            P(),
            P("tp", "pool"),
        ),
        out_specs=P("pool", "tp"),
        check_vma=False,
    )
```

```python
import functools
import math

import jax
import jax.numpy as jnp
import numpy as np
from jax import lax
from jax.experimental import pallas as pl
from jax.experimental.pallas import tpu as pltpu
from jax.sharding import PartitionSpec as P

rope_base = 1000000.0
CHUNK_BLOCKS = 16
MIB = 1024 * 1024
PROJ_MIB = 52
ATT_MIB = 2
ATT_VMEM = 32
EARLY_PIECES = 0
VMEM = pl.BlockSpec(memory_space=pltpu.VMEM)
SMEM = pl.BlockSpec(memory_space=pltpu.SMEM)
ANY = pl.BlockSpec(memory_space=pl.ANY)


def angle_tables(positions, head_dim):
    half_dim = head_dim // 2
    inverse = rope_base ** (-2.0 * np.arange(half_dim) / head_dim)
    angles = positions[:, None] * inverse[None, :]
    cosine, sine = np.cos(angles), np.sin(angles)
    return (
        np.concatenate([cosine, cosine], axis=1).astype(np.float32),
        np.concatenate([-sine, sine], axis=1).astype(np.float32),
    )


def add_angles(cos_a, sin_a, cos_b, sin_b):
    return cos_a * cos_b - sin_a * sin_b, sin_a * cos_b + cos_a * sin_b


def rope(values, cosine, sine):
    return values * cosine + pltpu.roll(values, values.shape[-1] // 2, 1) * sine


def table_rows(block_rows, base_count):
    return (
        slice(0, block_rows),
        slice(block_rows, 2 * block_rows),
        2 * block_rows,
        2 * block_rows + base_count,
    )


def send_kernel(
    place_ref,
    seats_ref,
    lengths_ref,
    map_ref,
    keys_ref,
    vals_ref,
    out_ref,
    held,
    plan,
    plan_scalar,
    in_sems,
    out_sems,
    plan_sem,
):
    count = held.shape[0]
    blocks_here, block_rows = keys_ref.shape[:2]
    block_count, sessions = map_ref.shape
    shift = blocks_here.bit_length() - 1
    lanes = plan.shape[1]

    lengths = lengths_ref[...].astype(jnp.float32)
    block = lax.broadcasted_iota(jnp.int32, (block_count, sessions), 0)
    here = ((block * block_rows).astype(jnp.float32) < lengths) & (
        map_ref[...] >> shift == place_ref[0]
    )
    code = (block * blocks_here + (map_ref[...] & (blocks_here - 1))).astype(jnp.float32)
    lowest = jnp.min(jnp.where(here, code, 1e6), axis=0, keepdims=True)
    highest = jnp.max(jnp.where(here, code, -1.0), axis=0, keepdims=True)
    number = jnp.sum(jnp.where(here, 1.0, 0.0), axis=0, keepdims=True)

    seat_row = seats_ref[...].astype(jnp.float32)
    down = lax.broadcasted_iota(jnp.int32, (sessions, sessions), 0)
    along = lax.broadcasted_iota(jnp.int32, (sessions, sessions), 1)
    seat_column = jnp.sum(jnp.where(down == along, seat_row, 0.0), axis=1, keepdims=True)
    seated = seat_column == along.astype(jnp.float32)
    down = lax.broadcasted_iota(jnp.int32, (sessions, lanes), 0)
    along = lax.broadcasted_iota(jnp.int32, (sessions, lanes), 1)

    def by_seat(row):
        column = jnp.sum(jnp.where(seated, row, 0.0), axis=1, keepdims=True)
        return jnp.sum(jnp.where(down == along, column, 0.0), axis=0, keepdims=True)

    low, high, num = by_seat(lowest), by_seat(highest), by_seat(number)
    low_next, high_next, num_next = (pltpu.roll(x, lanes - 1, 1) for x in (low, high, num))
    first = jnp.where(num >= 1.0, low, jnp.where(num_next >= 1.0, low_next, -1.0))
    second = jnp.where(
        num >= 2.0,
        high,
        jnp.where(
            num >= 1.0,
            jnp.where(num_next >= 1.0, low_next, -1.0),
            jnp.where(num_next >= 2.0, high_next, -1.0),
        ),
    )
    even = lax.broadcasted_iota(jnp.int32, (1, lanes), 1) % 2 == 0
    plan[...] = jnp.where(even, first, pltpu.roll(second, 1, 1)).astype(jnp.int32)
    to_scalar = pltpu.make_async_copy(plan, plan_scalar, plan_sem.at[0])
    to_scalar.start()
    to_scalar.wait()

    @pl.loop(0, count, unroll=4)
    def _(i):
        code = plan_scalar[0, i]

        @pl.when(code >= 0)
        def _():
            slot = code & (blocks_here - 1)
            pltpu.make_async_copy(keys_ref.at[slot], held.at[i, 0], in_sems.at[i]).start()
            pltpu.make_async_copy(vals_ref.at[slot], held.at[i, 1], in_sems.at[i]).start()

    @pl.loop(0, count, unroll=4)
    def _(i):
        code = plan_scalar[0, i]

        @pl.when(code >= 0)
        def _():
            pltpu.make_async_copy(held.at[i], held.at[i], in_sems.at[i]).wait()
            pltpu.make_async_copy(held.at[i], out_ref.at[i], out_sems.at[i]).start()

    @pl.loop(0, count, unroll=4)
    def _(i):
        @pl.when(plan_scalar[0, i] >= 0)
        def _():
            pltpu.make_async_copy(held.at[i], out_ref.at[i], out_sems.at[i]).wait()


def send_blocks(place, seats, lengths, map_t, pool_keys, pool_values, count):
    block_shape = pool_keys.shape[1:]
    return pl.pallas_call(
        send_kernel,
        out_shape=jax.ShapeDtypeStruct((count, 2) + block_shape, pool_keys.dtype),
        in_specs=[SMEM] + [VMEM] * 3 + [ANY] * 2,
        out_specs=ANY,
        scratch_shapes=[
            pltpu.VMEM((count, 2) + block_shape, pool_keys.dtype),
            pltpu.VMEM((1, 128), jnp.int32),
            pltpu.SMEM((1, 128), jnp.int32),
            pltpu.SemaphoreType.DMA((count,)),
            pltpu.SemaphoreType.DMA((count,)),
            pltpu.SemaphoreType.DMA((1,)),
        ],
        compiler_params=pltpu.CompilerParams(vmem_limit_bytes=60 * MIB),
        name="send_blocks",
    )(place, seats[None, :], lengths[None, :], map_t, pool_keys, pool_values)


def prepare_kernel(
    place_ref,
    seats_ref,
    lengths_ref,
    map_ref,
    tables,
    query_ref,
    key_ref,
    index_ref,
    own_ref,
    out_query_ref,
    out_key_ref,
    counts,
    *,
    base_count,
    blocks_here,
    capacity,
    block_rows,
):
    per_owner, heads, turn_len, head_dim = out_query_ref.shape
    block_count = index_ref.shape[1]
    shift = blocks_here.bit_length() - 1
    row_shift = block_rows.bit_length() - 1
    scaling = math.log2(math.e) / math.sqrt(head_dim)
    row_cos, row_sin, base_cos, base_sin = table_rows(block_rows, base_count)

    @pl.loop(0, counts.shape[0])
    def _(i):
        counts[i] = 0

    for seat in range(per_owner):
        session = seats_ref[place_ref[0] * per_owner + seat]
        length = lengths_ref[session]
        own_ref[seat] = length
        live = pl.cdiv(length, block_rows)

        @pl.loop(0, live)
        def _(j):
            source = map_ref[j, session] >> shift
            rank = counts[source]
            counts[source] = rank + 1
            index_ref[seat, j] = source * capacity + rank

        @pl.loop(live, block_count)
        def _(j):
            index_ref[seat, j] = index_ref[seat, 0]

        near = length & (block_rows - 1)
        far = length >> row_shift
        start_cos, start_sin = add_angles(
            tables[pl.ds(near, 1), :],
            tables[pl.ds(block_rows + near, 1), :],
            tables[pl.ds(base_cos + far, 1), :],
            tables[pl.ds(base_sin + far, 1), :],
        )
        for part in range(turn_len // block_rows):
            part_cos, part_sin = add_angles(
                start_cos,
                start_sin,
                tables[base_cos + part : base_cos + part + 1, :],
                tables[base_sin + part : base_sin + part + 1, :],
            )
            cosine, sine = add_angles(tables[row_cos, :], tables[row_sin, :], part_cos, part_sin)
            here = slice(part * block_rows, (part + 1) * block_rows)
            rows = slice(seat * turn_len + here.start, seat * turn_len + here.stop)
            key = key_ref[rows, :].astype(jnp.float32)
            out_key_ref[seat, here, :] = rope(key, cosine, sine).astype(jnp.bfloat16)
            cosine, sine = cosine * scaling, sine * scaling
            for h in range(heads):
                query = query_ref[rows, h * head_dim : (h + 1) * head_dim].astype(jnp.float32)
                out_query_ref[seat, h, here, :] = rope(query, cosine, sine).astype(jnp.bfloat16)


def prepare_turn(place, seats, lengths, map_t, table, base_count, turn_query, turn_key, sizes):
    pooled_count, blocks_here, capacity, per_owner, block_rows, head_dim = sizes
    turn_len = turn_query.shape[0] // per_owner
    heads = turn_query.shape[1] // head_dim
    block_count = map_t.shape[0]
    return pl.pallas_call(
        functools.partial(
            prepare_kernel,
            base_count=base_count,
            blocks_here=blocks_here,
            capacity=capacity,
            block_rows=block_rows,
        ),
        out_shape=(
            jax.ShapeDtypeStruct((per_owner, block_count), jnp.int32),
            jax.ShapeDtypeStruct((per_owner,), jnp.int32),
            jax.ShapeDtypeStruct((per_owner, heads, turn_len, head_dim), jnp.bfloat16),
            jax.ShapeDtypeStruct((per_owner, turn_len, head_dim), jnp.bfloat16),
        ),
        in_specs=[SMEM] * 4 + [VMEM] * 3,
        out_specs=(SMEM, SMEM, VMEM, VMEM),
        scratch_shapes=[pltpu.SMEM((pooled_count,), jnp.int32)],
        compiler_params=pltpu.CompilerParams(vmem_limit_bytes=16 * MIB),
        name="prepare_turn",
    )(place, seats, lengths, map_t, table, turn_query, turn_key)


def attention_kernel(
    seat,
    base_count,
    index_ref,
    length_ref,
    query_ref,
    turn_key_ref,
    turn_val_ref,
    tables,
    arrived_ref,
    out_ref,
    blocks,
    roped,
    top_ref,
    acc_ref,
    sems,
):
    _, heads, turn_len, head_dim = query_ref.shape
    _, _, block_rows, _ = blocks.shape
    chunk_rows = CHUNK_BLOCKS * block_rows
    length = length_ref[seat]
    chunks = pl.cdiv(length, chunk_rows)
    full = length // chunk_rows
    row_cos, row_sin, base_cos, base_sin = table_rows(block_rows, base_count)

    def copy(j):
        return pltpu.make_async_copy(arrived_ref.at[index_ref[seat, j]], blocks.at[j], sems.at[j])

    @pl.loop(0, chunks * CHUNK_BLOCKS, step=4)
    def _(j):
        for i in range(4):
            copy(j + i).start()

    def scores(h, keys):
        return lax.dot_general(
            query_ref[seat, h], keys, (((1,), (1,)), ((), ())), preferred_element_type=jnp.float32
        )

    def with_ones(vals):
        return jnp.concatenate([vals, jnp.ones(vals.shape, vals.dtype)], axis=1)

    rows = lax.broadcasted_iota(jnp.int32, (turn_len, turn_len), 0)
    cols = lax.broadcasted_iota(jnp.int32, (turn_len, turn_len), 1)
    new_keys = turn_key_ref[seat]
    new_vals = with_ones(turn_val_ref[seat * turn_len : (seat + 1) * turn_len, :])
    seen = [jnp.where(cols <= rows, scores(h, new_keys), -jnp.inf) for h in range(heads)]
    for h in range(heads):
        top = jnp.max(seen[h], axis=1, keepdims=True)
        weight = jnp.exp2(seen[h] - top).astype(jnp.bfloat16)
        top_ref[h] = top
        acc_ref[h] = jnp.dot(weight, new_vals, preferred_element_type=jnp.float32)

    def chunk_step(c, masked):
        first = c * CHUNK_BLOCKS

        @pl.loop(0, CHUNK_BLOCKS, step=4)
        def _(j):
            for i in range(4):
                copy(first + j + i).wait()

        for i in range(CHUNK_BLOCKS):
            cosine, sine = add_angles(
                tables[row_cos, :],
                tables[row_sin, :],
                tables[pl.ds(base_cos + first + i, 1), :],
                tables[pl.ds(base_sin + first + i, 1), :],
            )
            key = rope(blocks[first + i, 0].astype(jnp.float32), cosine, sine)
            roped[i * block_rows : (i + 1) * block_rows, :] = key.astype(jnp.bfloat16)
        keys = roped[...]
        vals = with_ones(blocks[pl.ds(first, CHUNK_BLOCKS), 1].reshape(chunk_rows, head_dim))
        seen = [scores(h, keys) for h in range(heads)]
        if masked:
            place = c * chunk_rows + lax.broadcasted_iota(jnp.int32, seen[0].shape, 1)
            seen = [jnp.where(place < length, s, -jnp.inf) for s in seen]
        for h in range(heads):
            old = top_ref[h]
            top = jnp.maximum(old, jnp.max(seen[h], axis=1, keepdims=True))
            weight = jnp.exp2(seen[h] - top).astype(jnp.bfloat16)
            fade = jnp.exp2(old - top)
            top_ref[h] = top
            acc_ref[h] = acc_ref[h] * fade + jnp.dot(
                weight, vals, preferred_element_type=jnp.float32
            )

    @pl.loop(0, full)
    def _(c):
        chunk_step(c, False)

    @pl.when(full < chunks)
    def _():
        chunk_step(full, True)

    for h in range(heads):
        acc = acc_ref[h]
        out_ref[:, h * head_dim : (h + 1) * head_dim] = (
            acc[:, :head_dim] / acc[:, head_dim:]
        ).astype(jnp.bfloat16)


def attend(seat, base_count, recv_index, lengths, query, turn_key, turn_val, table, arrived):
    _, heads, turn_len, head_dim = query.shape
    block_rows = arrived.shape[2]
    block_count = recv_index.shape[1]
    keys_seen = block_count * block_rows + turn_len
    return pl.pallas_call(
        functools.partial(attention_kernel, seat, base_count),
        out_shape=jax.ShapeDtypeStruct((turn_len, heads * head_dim), jnp.bfloat16),
        in_specs=[SMEM] * 2 + [VMEM] * 4 + [ANY],
        out_specs=VMEM,
        scratch_shapes=[
            pltpu.VMEM((block_count, 2, block_rows, head_dim), jnp.bfloat16),
            pltpu.VMEM((CHUNK_BLOCKS * block_rows, head_dim), jnp.bfloat16),
            pltpu.VMEM((heads, turn_len, 1), jnp.float32),
            pltpu.VMEM((heads, turn_len, 2 * head_dim), jnp.float32),
            pltpu.SemaphoreType.DMA((block_count,)),
        ],
        compiler_params=pltpu.CompilerParams(vmem_limit_bytes=ATT_VMEM * MIB),
        cost_estimate=pl.CostEstimate(
            flops=4 * heads * turn_len * keys_seen * head_dim,
            bytes_accessed=ATT_MIB * MIB,
            transcendentals=heads * turn_len * keys_seen,
        ),
        name="attend",
    )(recv_index, lengths, query, turn_key, turn_val, table, arrived)


def project_kernel(distances, started, place_ref, *refs):
    row_refs, refs = refs[:-5], refs[-5:]
    if started:
        row_refs, before_ref = row_refs[:-1], row_refs[-1]
    weight_ref, out_ref, held, rows, sems = refs
    pieces, _, width = held.shape
    depth = weight_ref.shape[1]
    count = len(distances)
    turn_len = row_refs[0].shape[0]
    tp = place_ref[0]
    groups = weight_ref.shape[0] // pieces

    def copy(i, j):
        home = weight_place(tp, (tp - distances[i]) & (groups - 1), j, pieces)
        return pltpu.make_async_copy(
            weight_ref.at[home], held.at[j, i * depth : (i + 1) * depth], sems.at[i, j]
        )

    for j in range(pieces):
        for i in range(count):
            copy(i, j).start()
    for k, row_ref in enumerate(row_refs):
        seat, i = divmod(k, count)
        rows[seat * turn_len : (seat + 1) * turn_len, i * depth : (i + 1) * depth] = row_ref[...]
    for j in range(pieces):
        for i in range(count):
            copy(i, j).wait()
        cols = slice(j * width, (j + 1) * width)
        for first in range(0, rows.shape[0], turn_len):
            here = slice(first, first + turn_len)
            part = jnp.dot(rows[here], held[j], preferred_element_type=jnp.float32)
            if started:
                part = part + before_ref[here, cols]
            out_ref[here, cols] = part.astype(out_ref.dtype)


def project(place, distances, gathered, before, weights, pieces, out_type):
    count = len(gathered[0])
    rows, depth = gathered[0][0].shape
    width = weights.shape[2]
    flat = [piece for seat in gathered for piece in seat]
    flat = flat if before is None else flat + [before]
    return pl.pallas_call(
        functools.partial(project_kernel, distances, before is not None),
        out_shape=jax.ShapeDtypeStruct((rows * len(gathered), pieces * width), out_type),
        in_specs=[SMEM] + [VMEM] * len(flat) + [pl.BlockSpec(memory_space=pltpu.HBM)],
        out_specs=VMEM,
        scratch_shapes=[
            pltpu.VMEM((pieces, count * depth, width), jnp.bfloat16),
            pltpu.VMEM((rows * len(gathered), count * depth), jnp.bfloat16),
            pltpu.SemaphoreType.DMA((count, pieces)),
        ],
        compiler_params=pltpu.CompilerParams(vmem_limit_bytes=PROJ_MIB * MIB),
        cost_estimate=pl.CostEstimate(
            flops=2 * rows * len(gathered) * count * depth * pieces * width,
            bytes_accessed=8 * MIB,
            transcendentals=0,
        ),
        name="project",
    )(place, *flat, weights)


def weight_place(plane, tp, rest, pieces):
    return ((plane ^ tp) * pieces + rest) ^ ((tp & 1) * (pieces // 2))


def spread_weights(out_weight, pieces):
    moves = []
    for p in range(lax.axis_size("pool")):
        for t in range(lax.axis_size("tp")):
            to = weight_place(p // pieces, t, p % pieces, pieces)
            moves.append((p * lax.axis_size("tp") + t, to * lax.axis_size("tp") + t))
    return lax.ppermute(out_weight, ("pool", "tp"), moves)


def to_planes(values, pieces):
    moves = []
    for p in range(lax.axis_size("pool")):
        for t in range(lax.axis_size("tp")):
            to = weight_place(p // pieces, t, p % pieces, pieces)
            moves.append((to * lax.axis_size("tp") + t, to * lax.axis_size("tp") + p // pieces))
    return lax.ppermute(values, ("pool", "tp"), moves)


def shift_tp(values, step):
    count = lax.axis_size("tp")
    return lax.ppermute(values, "tp", [(i, (i + step) % count) for i in range(count)])


def gather_ring(piece, farthest_from_left):
    count = lax.axis_size("tp")
    pieces, distances = [piece], [0]
    from_left = from_right = piece
    for distance in range(1, count // 2 + 1):
        last = 2 * distance == count
        if not last or farthest_from_left:
            from_left = shift_tp(from_left, 1)
            pieces.append(from_left)
            distances.append(distance)
        if not last or not farthest_from_left:
            from_right = shift_tp(from_right, -1)
            pieces.append(from_right)
            distances.append(-distance)
    return pieces, distances


def local(
    turn_query,
    turn_key,
    turn_value,
    pool_keys,
    pool_values,
    seat_session,
    history_len,
    block_map,
    out_weight,
):
    pooled_count = lax.axis_size("pool")
    tp_count = lax.axis_size("tp")
    place = lax.axis_index("pool")[None]
    blocks_here, rows_per_block, head_dim = pool_keys.shape
    block_count = block_map.shape[1]
    per_owner = seat_session.shape[0] // pooled_count
    capacity = per_owner * block_count // pooled_count
    pieces = pooled_count // tp_count

    base_count = block_count + 8
    table = jnp.asarray(
        np.concatenate(
            [
                *angle_tables(np.arange(rows_per_block), head_dim),
                *angle_tables(np.arange(base_count) * rows_per_block, head_dim),
            ]
        )
    )
    map_t = block_map.T

    spread = spread_weights(out_weight, pieces)
    sent = send_blocks(
        place,
        seat_session,
        history_len,
        map_t,
        pool_keys,
        pool_values,
        pooled_count * capacity,
    )
    sent, spread = lax.optimization_barrier((sent, spread))
    arrived = lax.all_to_all(sent, "pool", split_axis=0, concat_axis=0, tiled=True)

    turn_query, turn_key, _ = lax.optimization_barrier((turn_query, turn_key, sent))
    sizes = (pooled_count, blocks_here, capacity, per_owner, rows_per_block, head_dim)
    recv_index, own_lengths, queries, new_keys = prepare_turn(
        place, seat_session, history_len, map_t, table, base_count, turn_query, turn_key, sizes
    )
    moved = to_planes(spread, pieces)
    moved, arrived, queries = lax.optimization_barrier((moved, arrived, queries))
    weights = lax.all_gather(moved, "pool", axis=0, tiled=False)

    gathered = []
    for seat in range(per_owner):
        attended = attend(
            seat, base_count, recv_index, own_lengths, queries, new_keys, turn_value, table, arrived
        )
        if gathered:
            attended, *_ = lax.optimization_barrier((attended, *gathered[-1][1:3]))
        ring, distances = gather_ring(attended, seat % 2 == 0)
        gathered.append(ring)
    early = EARLY_PIECES
    where = lax.axis_index("tp")[None]
    if early == 0:
        return project(where, distances, gathered, None, weights, pieces, jnp.bfloat16)
    near, far = ([ring[:early] for ring in gathered], [ring[early:] for ring in gathered])
    partial = project(where, distances[:early], near, None, weights, pieces, jnp.float32)
    return project(where, distances[early:], far, partial, weights, pieces, jnp.bfloat16)


def solution(mesh):
    return jax.shard_map(
        local,
        mesh=mesh,
        in_specs=(
            P("pool", "tp"),
            P("pool", "tp"),
            P("pool", "tp"),
            P("pool", None, "tp"),
            P("pool", None, "tp"),
            P(),
            P(),
            P(),
            P("tp", "pool"),
        ),
        out_specs=P("pool", "tp"),
        check_vma=False,
    )
```
